32 devices in a mesh: groups: 2 (over y), pairs: 8 (over z, x), rows: 2 (over core).
Axes of the slice: x: 2, y: 2, z: 4, core: 2. Of those that a mesh axis runs over, the one named last changes fastest.
Arguments:
- images: bfloat16 [128, 16, 768], P('groups', ('pairs', 'rows')), parts along dimension 0, may hold values from -12 to 12
- w_qkv: bfloat16 [768, 2304], replicated, may hold values from -0.21875 to 0.21875
- w_out: bfloat16 [768, 768], replicated, may hold values from -0.21875 to 0.21875
- pair_list: int32 [48, 2], P('groups'), parts along dimension 0, may hold values from 0 to 63, as said below
- pair_weight: int32 [48], P('groups'), parts along dimension 0, may hold values from 0 to 4, as said below
Outputs:
- mixed: bfloat16 [128, 16, 768], P('groups', ('pairs', 'rows')), parts along dimension 0
The draws below stay inside these ranges and needn't reach their ends.
There are 2 independent parts, one for each index of `groups`. The reference program is written for one: setup_inputs(seed, part) draws one part's arguments, and reference() takes and returns one part's arrays. A program takes and returns all parts, laid end to end along the dimension named above; an argument that names none is the same for every part. Nothing has to cross between parts.
Inputs may be any that keep to these rules, and one draw needn't show every extreme that they name: `pair_list`: the two images of a slot differ. `pair_weight`: A slot is live when its weight is positive. Slots 3 * g to 3 * g + 2 form pair group g, and group g belongs to device g along pairs. Exactly 16 slots are live, and in every draw some group has all 3 slots live.
All inputs are finite; a program needn't handle non-finite values.
Results may differ from the reference program's by a relative error of at most 0.0034.
Values may be sent and summed in bfloat16 or wider, within the bound.
A program may use at most 64 MiB of HBM per device.

```python
import jax
import jax.numpy as jnp
from jax import lax

D = 768
HEADS = 12
HDIM = 64
IMGS = 64
PMAX = 3
TOK = 16
SLOTS = 24
LIVE = 16
N_PAIRS = 8


def draw_images(key, part):
    first = jax.random.fold_in(key, 0)
    return jnp.clip(jax.random.normal(first, (IMGS, TOK, D), jnp.float32), -4.0, 4.0).astype(jnp.bfloat16)


def draw_pair_list(key, part):
    first, second = jax.random.split(jax.random.fold_in(key, 11))
    left_end = jax.random.randint(first, (SLOTS,), 0, IMGS)
    stride = jax.random.randint(second, (SLOTS,), 1, IMGS)
    right_end = (left_end + stride) % IMGS
    return jnp.stack([left_end, right_end], axis=1).astype(jnp.int32)


def draw_pair_weight(key, part):
    first, second, third = jax.random.split(jax.random.fold_in(key, 23), 3)
    ranks = jax.random.permutation(first, SLOTS).astype(jnp.int32)
    chosen = jax.random.randint(second, (), 0, N_PAIRS)
    member_group = jnp.arange(SLOTS, dtype=jnp.int32) // PMAX
    score = ranks + SLOTS * (member_group == chosen).astype(jnp.int32)
    ranking = jnp.argsort(-score)
    active = jnp.zeros((SLOTS,), jnp.int32).at[ranking[:LIVE]].set(1)
    levels = jax.random.randint(third, (SLOTS,), 1, 5)
    return (active * levels).astype(jnp.int32)


def gaussian(own_key, dims, deviation, reach, kind=jnp.bfloat16):
    entries = jax.random.normal(own_key, dims, jnp.float32) * deviation
    return jnp.minimum(jnp.maximum(entries, -reach), reach).astype(kind)


def setup_inputs(seed: int = 0, part: int = 0) -> dict:
    splits = jax.random.split(jax.random.key(seed), 6)
    own_keys = jax.random.split(jax.random.fold_in(splits[5], part), 6)
    images = draw_images(jax.random.fold_in(jax.random.fold_in(splits[5], part), 71), part)
    w_qkv = gaussian(splits[1], (D, 3 * D), D ** -0.5, 0.21875)
    w_out = gaussian(splits[2], (D, D), D ** -0.5, 0.21875)
    pair_list = draw_pair_list(jax.random.fold_in(jax.random.fold_in(splits[5], part), 71), part)
    pair_weight = draw_pair_weight(jax.random.fold_in(jax.random.fold_in(splits[5], part), 71), part)
    return dict(images=images, w_qkv=w_qkv, w_out=w_out, pair_list=pair_list, pair_weight=pair_weight)


def attend(queries, key_rows, value_rows):
    tokens_q = queries.shape[0]
    tokens_k = key_rows.shape[0]
    split_q = queries.astype(jnp.float32).reshape(tokens_q, HEADS, HDIM)
    split_k = key_rows.astype(jnp.float32).reshape(tokens_k, HEADS, HDIM)
    split_v = value_rows.astype(jnp.float32).reshape(tokens_k, HEADS, HDIM)
    scores = jnp.einsum("qhc,shc->hqs", split_q, split_k) * (HDIM ** -0.5)
    largest = jnp.max(scores, axis=2, keepdims=True)
    exponent = jnp.exp(scores - largest)
    softmax = (exponent / jnp.sum(exponent, axis=2, keepdims=True)).astype(jnp.bfloat16)
    softmax = lax.optimization_barrier(softmax).astype(jnp.float32)
    blended = jnp.einsum("hqs,shc->qhc", softmax, split_v)
    return blended.reshape(tokens_q, HEADS * HDIM)


def reference(images, w_qkv, w_out, pair_list, pair_weight):
    projected = jnp.dot(images.reshape(IMGS * TOK, D), w_qkv, preferred_element_type=jnp.float32)
    projected = projected.astype(jnp.bfloat16).reshape(IMGS, TOK, 3 * D)

    def one_slot(summed, slot_index):
        pair_ends = pair_list[slot_index]
        factor = pair_weight[slot_index].astype(jnp.float32)

        def add_live(running):
            for end_index in range(2):
                source = projected[pair_ends[end_index]]
                partner = projected[pair_ends[1 - end_index]]
                attended = attend(source[:, :D], partner[:, D:2 * D], partner[:, 2 * D:])
                message = (attended * factor).astype(jnp.bfloat16)
                message = lax.optimization_barrier(message).astype(jnp.float32)
                running = running.at[pair_ends[end_index]].add(message)
            return running

        return lax.cond(factor > 0, add_live, lambda member: member, summed), None

    summed, unused = lax.scan(one_slot, jnp.zeros((IMGS, TOK, D), jnp.float32), jnp.arange(SLOTS, dtype=jnp.int32))
    matches = (pair_list[None, :, :] == jnp.arange(IMGS, dtype=jnp.int32)[:, None, None]).astype(jnp.float32)
    totals = 1.0 + jnp.sum(matches * pair_weight.astype(jnp.float32)[None, :, None], axis=(1, 2))
    average = (summed / totals[:, None, None]).astype(jnp.bfloat16)
    update = jnp.dot(average.reshape(IMGS * TOK, D), w_out, preferred_element_type=jnp.float32)
    result = images.reshape(IMGS * TOK, D).astype(jnp.float32) + update
    return result.astype(jnp.bfloat16).reshape(IMGS, TOK, D)
```

```python
import functools

import jax
import jax.numpy as jnp
from jax import lax
from jax.experimental import pallas as pl
from jax.experimental.pallas import tpu as pltpu
from jax.sharding import PartitionSpec as P

HDIM = 64
LANES = 128
ROWS = 16
F32 = jnp.float32
BF16 = jnp.bfloat16


def iota(shape, axis):
    return lax.broadcasted_iota(jnp.int32, shape, axis)


def onehot(mask):
    return jnp.where(mask, 1.0, 0.0).astype(BF16)


def dot(a, b):
    return jnp.dot(a, b, preferred_element_type=F32)


def each_chunk(count, body):
    if count == 1:
        body(0)
    else:
        lax.fori_loop(0, count, lambda i, c: (body(i), c)[1], 0)


def rows_at(start, size):
    if isinstance(start, int):
        return pl.ds(start, size)
    return pl.ds(pl.multiple_of(start, ROWS), size)


def kernel(
    n, row_devices, img_hbm, wq_hbm, wo_hbm, ends_ref, weight_ref, out_ref,
    img, wq, wo, send, recv, send2, recv2, proj, stack, combine,
    load_sem, send_sem, recv_sem,
):
    imgs, d = img.shape
    slots = ends_ref.shape[1]
    col_blocks = d // LANES
    chunks = n // ROWS
    block = ROWS * ROWS
    pairs_pos = lax.axis_index("pairs")
    rows_pos = lax.axis_index("rows")
    me = pairs_pos * row_devices + rows_pos

    loads = [
        pltpu.make_async_copy(src, dst, load_sem.at[i])
        for i, (src, dst) in enumerate([(img_hbm, img), (wq_hbm, wq), (wo_hbm, wo)])
    ]
    for load in loads:
        load.start()

    def partner(step):
        other = lax.rem(me + step, n)
        return other, {"pairs": other // row_devices, "rows": lax.rem(other, row_devices)}

    barrier = pltpu.get_barrier_semaphore()

    def greet(step, carry):
        pl.semaphore_signal(
            barrier, inc=1, device_id=partner(step)[1], device_id_type=pl.DeviceIdType.MESH
        )
        return carry

    lax.fori_loop(1, n, greet, 0)

    sub = iota((slots, slots), 0)
    lane = iota((slots, slots), 1)
    w_row = weight_ref[...].astype(F32)
    w_col = jnp.sum(jnp.where(sub == lane, w_row, 0.0), axis=1, keepdims=True)
    ends = ends_ref[...].astype(F32)
    end_row = [ends[e:e + 1] for e in range(2)]
    end_col = [
        jnp.sum(jnp.where(sub == lane, row, 0.0), axis=1, keepdims=True) for row in end_row
    ]
    live_row = jnp.where(w_row > 0, 1.0, 0.0)
    live_col = jnp.where(w_col > 0, 1.0, 0.0)
    rank_row = jnp.sum(jnp.where(sub < lane, live_col, 0.0), axis=0, keepdims=True)
    rank_col = jnp.sum(jnp.where(lane < sub, live_row, 0.0), axis=1, keepdims=True)
    rank_row = jnp.where(w_row > 0, rank_row, -1.0)
    rank_col = jnp.where(w_col > 0, rank_col, -1.0)

    loads[0].wait()
    image_stack = jnp.concatenate(
        [img[:, c * LANES:(c + 1) * LANES] for c in range(col_blocks)], axis=0
    )
    per_tile = LANES // imgs

    def fill(ch):
        row = iota((block, 1), 0)
        place = (row // ROWS + ch * ROWS).astype(F32)
        kind = row % ROWS
        chosen = jnp.where(kind >= col_blocks, end_row[1], end_row[0])
        image = jnp.sum(jnp.where(rank_row == place, chosen, 0.0), axis=1, keepdims=True)
        column = jnp.where(kind >= col_blocks, kind - col_blocks, kind)
        column = jnp.where(kind >= 2 * col_blocks, -1, column)
        across = iota((1, LANES), 1)
        which = (across % imgs).astype(F32)
        parts = [
            onehot((image == which) & (column == m * per_tile + across // imgs))
            for m in range(col_blocks // per_tile)
        ]
        picked = dot(jnp.concatenate(parts, axis=1), image_stack)
        send[rows_at(ch * block, block), :] = picked.astype(BF16)

    each_chunk(chunks, fill)

    pl.semaphore_wait(barrier, n - 1)

    def exchange(source, target, which):
        def one(step, carry):
            other, where = partner(step)
            pltpu.make_async_remote_copy(
                src_ref=source.at[rows_at(other * ROWS, ROWS)],
                dst_ref=target.at[rows_at(me * ROWS, ROWS)],
                send_sem=send_sem.at[which],
                recv_sem=recv_sem.at[which],
                device_id=where,
                device_id_type=pl.DeviceIdType.MESH,
            ).start()
            return carry

        lax.fori_loop(1, n, one, 0)
        target[rows_at(me * ROWS, ROWS), :] = source[rows_at(me * ROWS, ROWS), :]

    def await_all(buffer, sem):
        whole = buffer.at[pl.ds(0, (n - 1) * ROWS)]
        pltpu.make_async_copy(whole, whole, sem).wait()

    exchange(send, recv, 0)

    def fill_combine(ch):
        across = iota((1, block), 1)
        place = (across // ROWS + ch * ROWS).astype(F32)
        kind = across % ROWS
        chosen = jnp.where(kind >= col_blocks, end_col[1], end_col[0])
        image = jnp.sum(jnp.where(rank_col == place, chosen, 0.0), axis=0, keepdims=True)
        column = jnp.where(kind >= col_blocks, kind - col_blocks, kind)
        column = jnp.where(kind >= 2 * col_blocks, -1, column)
        same = image == iota((imgs, 1), 0).astype(F32)
        for c in range(col_blocks):
            combine[ch, c * imgs:(c + 1) * imgs, :] = onehot(same & (column == c))

    each_chunk(chunks, fill_combine)
    number = iota((imgs, 1), 0).astype(F32)
    totals = 1.0 + jnp.sum(
        jnp.where(end_row[0] == number, w_row, 0.0) + jnp.where(end_row[1] == number, w_row, 0.0),
        axis=1, keepdims=True,
    )
    my_weight = jnp.sum(
        jnp.where(rank_row == me.astype(F32), w_row, 0.0), axis=1, keepdims=True
    )
    height = 2 * ROWS * col_blocks

    def spot(row):
        return (row % ROWS) * ROWS + (row // ROWS % 2) * col_blocks + row // (2 * ROWS)

    unpack = onehot(spot(iota((height, 1), 0)) == iota((1, block), 1))
    pack = onehot(spot(iota((1, height), 1)) == iota((block, 1), 0))
    head_of = iota((1, 4 * HDIM), 1) // HDIM
    heads = [onehot(head_of == h) for h in range(4)]
    heads32 = [jnp.where(head_of == h, 1.0, 0.0) for h in range(4)]

    await_all(recv, recv_sem.at[0])
    loads[1].wait()

    def project(ch):
        tokens = dot(unpack, recv[rows_at(ch * block, block), :]).astype(BF16)
        tokens = jnp.concatenate(
            [tokens[c * 2 * ROWS:(c + 1) * 2 * ROWS] for c in range(col_blocks)], axis=1
        )
        for part in range(3):
            result = dot(tokens, wq[:, part * d:(part + 1) * d]).astype(BF16)
            for e in range(2):
                proj[rows_at(e * n + ch * ROWS, ROWS), part * d:(part + 1) * d] = (
                    result[e * ROWS:(e + 1) * ROWS]
                )

    each_chunk(chunks, project)

    def attend(ch):
        for e in range(2):
            for b in range(d // (4 * HDIM)):
                lo = b * 4 * HDIM
                hi = lo + 4 * HDIM
                query = proj[rows_at(e * n + ch * ROWS, ROWS), lo:hi]
                keys = proj[(1 - e) * n:(2 - e) * n, d + lo:d + hi]
                values = proj[(1 - e) * n:(2 - e) * n, 2 * d + lo:2 * d + hi]
                split = jnp.concatenate([query * mask for mask in heads], axis=0)
                scores = lax.dot_general(
                    split, keys, (((1,), (1,)), ((), ())), preferred_element_type=F32
                ) * HDIM ** (-0.5)
                largest = jnp.max(scores, axis=1, keepdims=True)
                exponent = jnp.exp(scores - largest)
                softmax = (exponent / jnp.sum(exponent, axis=1, keepdims=True)).astype(BF16)
                blended = dot(softmax, values)
                attended = sum(
                    blended[h * ROWS:(h + 1) * ROWS] * heads32[h] for h in range(4)
                )
                message = (attended * my_weight).astype(BF16)
                for half in range(2):
                    c = 2 * b + half
                    stack[c * 2 * ROWS + e * ROWS:c * 2 * ROWS + (e + 1) * ROWS, :] = (
                        message[:, half * LANES:(half + 1) * LANES]
                    )
        send2[rows_at(ch * block, block), :] = dot(pack, stack[...]).astype(BF16)

    each_chunk(chunks, attend)

    exchange(send2, recv2, 1)
    loads[2].wait()
    await_all(send, send_sem.at[0])
    await_all(recv2, recv_sem.at[1])

    def add_up(ch):
        return dot(combine[ch], recv2[rows_at(ch * block, block), :])

    if chunks == 1:
        summed = add_up(0)
    else:
        summed = lax.fori_loop(
            1, chunks, lambda ch, total: total + add_up(ch), add_up(0)
        )
    average = jnp.concatenate(
        [(summed[c * imgs:(c + 1) * imgs] / totals).astype(BF16) for c in range(col_blocks)],
        axis=1,
    )
    update = dot(average, wo[...])
    out_ref[...] = (img[...].astype(F32) + update).astype(BF16)
    await_all(send2, send_sem.at[1])


def local(images, w_qkv, w_out, pair_list, pair_weight):
    row_devices = lax.axis_size("rows")
    n = lax.axis_size("pairs") * row_devices
    imgs, local_tokens, d = images.shape
    assert local_tokens == 1 and n % ROWS == 0
    slots = pair_list.shape[0]
    any_space = pl.BlockSpec(memory_space=pl.ANY)
    vmem = pl.BlockSpec(memory_space=pltpu.VMEM)
    col_blocks = d // LANES
    buffer = pltpu.VMEM((n * ROWS, LANES), BF16)
    flat = images.reshape(imgs, d)
    result = pl.pallas_call(
        functools.partial(kernel, n, row_devices),
        out_shape=jax.ShapeDtypeStruct((imgs, d), BF16),
        in_specs=[any_space, any_space, any_space, vmem, vmem],
        out_specs=vmem,
        scratch_shapes=[
            pltpu.VMEM((imgs, d), BF16),
            pltpu.VMEM(w_qkv.shape, BF16),
            pltpu.VMEM(w_out.shape, BF16),
            buffer, buffer, buffer, buffer,
            pltpu.VMEM((2 * n, 3 * d), BF16),
            pltpu.VMEM((2 * ROWS * col_blocks, LANES), BF16),
            pltpu.VMEM((n // ROWS, imgs * col_blocks, ROWS * ROWS), BF16),
            pltpu.SemaphoreType.DMA((3,)),
            pltpu.SemaphoreType.DMA((2,)),
            pltpu.SemaphoreType.DMA((2,)),
        ],
        compiler_params=pltpu.CompilerParams(
            collective_id=0, has_side_effects=True, vmem_limit_bytes=56 * 1024 * 1024
        ),
    )(flat, w_qkv, w_out, pair_list.T, pair_weight.reshape(1, slots))
    return result.reshape(images.shape)


def solution(mesh):
    in_specs = (P("groups", ("pairs", "rows"), None), P(), P(), P("groups", None), P("groups"))
    out_specs = P("groups", ("pairs", "rows"), None)
    return jax.shard_map(local, mesh=mesh, in_specs=in_specs, out_specs=out_specs, check_vma=False)
```

```python
import functools

import jax
import jax.numpy as jnp
from jax import lax
from jax.experimental import pallas as pl
from jax.experimental.pallas import tpu as pltpu
from jax.sharding import PartitionSpec as P

HDIM = 64
LANES = 128
ROWS = 16
F32 = jnp.float32
BF16 = jnp.bfloat16


def iota(shape, axis):
    return lax.broadcasted_iota(jnp.int32, shape, axis)


def onehot(mask):
    return jnp.where(mask, 1.0, 0.0).astype(BF16)


def dot(a, b):
    return jnp.dot(a, b, preferred_element_type=F32)


def each_chunk(count, body):
    if count == 1:
        body(0)
    else:
        lax.fori_loop(0, count, lambda i, c: (body(i), c)[1], 0)


def rows_at(start, size):
    if isinstance(start, int):
        return pl.ds(start, size)
    return pl.ds(pl.multiple_of(start, ROWS), size)


def kernel(
    n, row_devices, img_hbm, wq_hbm, ends_hbm, weight_hbm, out_ref,
    ends_ref, weight_ref, img, wq, send, recv, send2, recv2, proj, stack, combine,
    load_sem, send_sem, recv_sem,
):
    imgs, d = img.shape
    slots = ends_ref.shape[1]
    col_blocks = d // LANES
    chunks = n // ROWS
    block = ROWS * ROWS
    pairs_pos = lax.axis_index("pairs")
    rows_pos = lax.axis_index("rows")
    me = pairs_pos * row_devices + rows_pos

    pairs_of_refs = [
        (ends_hbm, ends_ref), (weight_hbm, weight_ref), (img_hbm, img), (wq_hbm, wq)
    ]
    loads = [
        pltpu.make_async_copy(src, dst, load_sem.at[i])
        for i, (src, dst) in enumerate(pairs_of_refs)
    ]

    def partner(step):
        other = me
        bit = 1
        while bit < n:
            other = other + (step // bit % 2) * (1 - 2 * (me // bit % 2)) * bit
            bit *= 2
        return other, {"pairs": other // row_devices, "rows": lax.rem(other, row_devices)}

    def each_partner(body):
        if chunks == 1:
            for step in range(n - 1, 0, -1):
                body(step, 0)
        else:
            lax.fori_loop(1, n, lambda i, c: body(n - i, c), 0)

    barrier = pltpu.get_barrier_semaphore()

    def greet(step, carry):
        pl.semaphore_signal(
            barrier, inc=1, device_id=partner(step)[1], device_id_type=pl.DeviceIdType.MESH
        )
        return carry

    each_partner(greet)

    for load in loads:
        load.start()

    loads[0].wait()
    loads[1].wait()

    sub = iota((slots, slots), 0)
    lane = iota((slots, slots), 1)
    w_row = weight_ref[...].astype(F32)
    w_col = jnp.sum(jnp.where(sub == lane, w_row, 0.0), axis=1, keepdims=True)
    ends = ends_ref[...].astype(F32)
    end_row = [ends[e:e + 1] for e in range(2)]
    end_col = [
        jnp.sum(jnp.where(sub == lane, row, 0.0), axis=1, keepdims=True) for row in end_row
    ]
    live_row = jnp.where(w_row > 0, 1.0, 0.0)
    live_col = jnp.where(w_col > 0, 1.0, 0.0)
    rank_row = jnp.sum(jnp.where(sub < lane, live_col, 0.0), axis=0, keepdims=True)
    rank_col = jnp.sum(jnp.where(lane < sub, live_row, 0.0), axis=1, keepdims=True)
    rank_row = jnp.where(w_row > 0, rank_row, -1.0)
    rank_col = jnp.where(w_col > 0, rank_col, -1.0)

    loads[2].wait()
    image_stack = jnp.concatenate(
        [img[:, c * LANES:(c + 1) * LANES] for c in range(col_blocks)], axis=0
    )
    per_tile = LANES // imgs

    def fill(ch):
        row = iota((block, 1), 0)
        place = (row // ROWS + ch * ROWS).astype(F32)
        kind = row % ROWS
        chosen = jnp.where(kind >= col_blocks, end_row[1], end_row[0])
        image = jnp.sum(jnp.where(rank_row == place, chosen, 0.0), axis=1, keepdims=True)
        column = jnp.where(kind >= col_blocks, kind - col_blocks, kind)
        column = jnp.where(kind >= 2 * col_blocks, -1, column)
        across = iota((1, LANES), 1)
        which = (across % imgs).astype(F32)
        parts = [
            onehot((image == which) & (column == m * per_tile + across // imgs))
            for m in range(col_blocks // per_tile)
        ]
        picked = dot(jnp.concatenate(parts, axis=1), image_stack)
        send[rows_at(ch * block, block), :] = picked.astype(BF16)

    each_chunk(chunks, fill)

    pl.semaphore_wait(barrier, n - 1)

    def exchange(source, target, which):
        def one(step, carry):
            other, where = partner(step)
            pltpu.make_async_remote_copy(
                src_ref=source.at[rows_at(other * ROWS, ROWS)],
                dst_ref=target.at[rows_at(me * ROWS, ROWS)],
                send_sem=send_sem.at[which],
                recv_sem=recv_sem.at[which],
                device_id=where,
                device_id_type=pl.DeviceIdType.MESH,
            ).start()
            return carry

        each_partner(one)
        target[rows_at(me * ROWS, ROWS), :] = source[rows_at(me * ROWS, ROWS), :]

    def await_all(buffer, sem):
        whole = buffer.at[pl.ds(0, (n - 1) * ROWS)]
        pltpu.make_async_copy(whole, whole, sem).wait()

    exchange(send, recv, 0)

    def fill_combine(ch):
        across = iota((1, block), 1)
        place = (across // ROWS + ch * ROWS).astype(F32)
        kind = across % ROWS
        chosen = jnp.where(kind >= col_blocks, end_col[1], end_col[0])
        image = jnp.sum(jnp.where(rank_col == place, chosen, 0.0), axis=0, keepdims=True)
        column = jnp.where(kind >= col_blocks, kind - col_blocks, kind)
        column = jnp.where(kind >= 2 * col_blocks, -1, column)
        same = image == iota((imgs, 1), 0).astype(F32)
        for c in range(col_blocks):
            combine[ch, c * imgs:(c + 1) * imgs, :] = onehot(same & (column == c))

    each_chunk(chunks, fill_combine)
    number = iota((imgs, 1), 0).astype(F32)
    totals = 1.0 + jnp.sum(
        jnp.where(end_row[0] == number, w_row, 0.0) + jnp.where(end_row[1] == number, w_row, 0.0),
        axis=1, keepdims=True,
    )
    my_weight = jnp.sum(
        jnp.where(rank_row == me.astype(F32), w_row, 0.0), axis=1, keepdims=True
    )
    height = 2 * ROWS * col_blocks

    def spot(row):
        return (row % ROWS) * ROWS + (row // ROWS % 2) * col_blocks + row // (2 * ROWS)

    unpack = onehot(spot(iota((height, 1), 0)) == iota((1, block), 1))
    pack = onehot(spot(iota((1, height), 1)) == iota((block, 1), 0))
    head_of = iota((1, 4 * HDIM), 1) // HDIM
    heads = [onehot(head_of == h) for h in range(4)]
    heads32 = [jnp.where(head_of == h, 1.0, 0.0) for h in range(4)]

    await_all(recv, recv_sem.at[0])
    loads[3].wait()

    def project(ch):
        tokens = dot(unpack, recv[rows_at(ch * block, block), :]).astype(BF16)
        tokens = jnp.concatenate(
            [tokens[c * 2 * ROWS:(c + 1) * 2 * ROWS] for c in range(col_blocks)], axis=1
        )
        for part in range(3):
            result = dot(tokens, wq[:, part * d:(part + 1) * d]).astype(BF16)
            for e in range(2):
                proj[rows_at(e * n + ch * ROWS, ROWS), part * d:(part + 1) * d] = (
                    result[e * ROWS:(e + 1) * ROWS]
                )

    each_chunk(chunks, project)

    def attend(ch):
        for e in range(2):
            for b in range(d // (4 * HDIM)):
                lo = b * 4 * HDIM
                hi = lo + 4 * HDIM
                query = proj[rows_at(e * n + ch * ROWS, ROWS), lo:hi]
                keys = proj[(1 - e) * n:(2 - e) * n, d + lo:d + hi]
                values = proj[(1 - e) * n:(2 - e) * n, 2 * d + lo:2 * d + hi]
                split = jnp.concatenate([query * mask for mask in heads], axis=0)
                scores = lax.dot_general(
                    split, keys, (((1,), (1,)), ((), ())), preferred_element_type=F32
                ) * HDIM ** (-0.5)
                largest = jnp.max(scores, axis=1, keepdims=True)
                exponent = jnp.exp(scores - largest)
                softmax = (exponent / jnp.sum(exponent, axis=1, keepdims=True)).astype(BF16)
                blended = dot(softmax, values)
                attended = sum(
                    blended[h * ROWS:(h + 1) * ROWS] * heads32[h] for h in range(4)
                )
                message = (attended * my_weight).astype(BF16)
                for half in range(2):
                    c = 2 * b + half
                    stack[c * 2 * ROWS + e * ROWS:c * 2 * ROWS + (e + 1) * ROWS, :] = (
                        message[:, half * LANES:(half + 1) * LANES]
                    )
        send2[rows_at(ch * block, block), :] = dot(pack, stack[...]).astype(BF16)

    each_chunk(chunks, attend)

    exchange(send2, recv2, 1)
    await_all(send, send_sem.at[0])
    await_all(recv2, recv_sem.at[1])

    def add_up(ch):
        return dot(combine[ch], recv2[rows_at(ch * block, block), :])

    if chunks == 1:
        summed = add_up(0)
    else:
        summed = lax.fori_loop(
            1, chunks, lambda ch, total: total + add_up(ch), add_up(0)
        )
    average = jnp.concatenate(
        [(summed[c * imgs:(c + 1) * imgs] / totals).astype(BF16) for c in range(col_blocks)],
        axis=1,
    )
    out_ref[...] = average
    await_all(send2, send_sem.at[1])


def local(images, w_qkv, w_out, pair_list, pair_weight):
    row_devices = lax.axis_size("rows")
    n = lax.axis_size("pairs") * row_devices
    imgs, local_tokens, d = images.shape
    assert local_tokens == 1 and n % ROWS == 0
    slots = pair_list.shape[0]
    any_space = pl.BlockSpec(memory_space=pl.ANY)
    vmem = pl.BlockSpec(memory_space=pltpu.VMEM)
    col_blocks = d // LANES
    buffer = pltpu.VMEM((n * ROWS, LANES), BF16)
    flat = images.reshape(imgs, d)
    result = pl.pallas_call(
        functools.partial(kernel, n, row_devices),
        out_shape=pltpu.VMEM((imgs, d), BF16),
        in_specs=[any_space] * 4,
        out_specs=vmem,
        scratch_shapes=[
            pltpu.VMEM((2, slots), jnp.int32),
            pltpu.VMEM((1, slots), jnp.int32),
            pltpu.VMEM((imgs, d), BF16),
            pltpu.VMEM(w_qkv.shape, BF16),
            buffer, buffer, buffer, buffer,
            pltpu.VMEM((2 * n, 3 * d), BF16),
            pltpu.VMEM((2 * ROWS * col_blocks, LANES), BF16),
            pltpu.VMEM((n // ROWS, imgs * col_blocks, ROWS * ROWS), BF16),
            pltpu.SemaphoreType.DMA((4,)),
            pltpu.SemaphoreType.DMA((2,)),
            pltpu.SemaphoreType.DMA((2,)),
        ],
        compiler_params=pltpu.CompilerParams(
            collective_id=0, has_side_effects=True, vmem_limit_bytes=56 * 1024 * 1024
        ),
    )(flat, w_qkv, pair_list.T, pair_weight.reshape(1, slots))
    update = jnp.dot(result, w_out, preferred_element_type=F32)
    return (flat.astype(F32) + update).astype(BF16).reshape(images.shape)


def solution(mesh):
    in_specs = (P("groups", ("pairs", "rows"), None), P(), P(), P("groups", None), P("groups"))
    out_specs = P("groups", ("pairs", "rows"), None)
    return jax.shard_map(local, mesh=mesh, in_specs=in_specs, out_specs=out_specs, check_vma=False)
```

```python
import functools

import jax
import jax.numpy as jnp
from jax import lax
from jax.experimental import pallas as pl
from jax.experimental.pallas import tpu as pltpu
from jax.sharding import PartitionSpec as P

HDIM = 64
LANES = 128
ROWS = 16
F32 = jnp.float32
BF16 = jnp.bfloat16


def iota(shape, axis):
    return lax.broadcasted_iota(jnp.int32, shape, axis)


def onehot(mask):
    return jnp.where(mask, 1.0, 0.0).astype(BF16)


def dot(a, b):
    return jnp.dot(a, b, preferred_element_type=F32)


def each_chunk(count, body):
    if count == 1:
        body(0)
    else:
        lax.fori_loop(0, count, lambda i, c: (body(i), c)[1], 0)


def rows_at(start, size):
    if isinstance(start, int):
        return pl.ds(start, size)
    return pl.ds(pl.multiple_of(start, ROWS), size)


def kernel(
    n, row_devices, img_hbm, wq_hbm, ends_hbm, weight_hbm, out_ref,
    ends_ref, weight_ref, img, wq, send, recv, send2, recv2, proj, stack, combine,
    load_sem, send_sem, recv_sem,
):
    imgs, d = img.shape
    slots = ends_ref.shape[1]
    col_blocks = d // LANES
    chunks = n // ROWS
    block = ROWS * ROWS
    pairs_pos = lax.axis_index("pairs")
    rows_pos = lax.axis_index("rows")
    me = pairs_pos * row_devices + rows_pos

    pairs_of_refs = [
        (ends_hbm, ends_ref), (weight_hbm, weight_ref), (img_hbm, img), (wq_hbm, wq)
    ]
    loads = [
        pltpu.make_async_copy(src, dst, load_sem.at[i])
        for i, (src, dst) in enumerate(pairs_of_refs)
    ]

    def partner(step):
        other = me
        bit = 1
        while bit < n:
            other = other + (step // bit % 2) * (1 - 2 * (me // bit % 2)) * bit
            bit *= 2
        return other, {"pairs": other // row_devices, "rows": lax.rem(other, row_devices)}

    def each_partner(body):
        if chunks == 1:
            for step in range(n - 1, 0, -1):
                body(step, 0)
        else:
            lax.fori_loop(1, n, lambda i, c: body(n - i, c), 0)

    barrier = pltpu.get_barrier_semaphore()

    workers = n // 2
    first = n // 4

    def works(device):
        return (device >= first) & (device < first + workers)

    i_work = works(me)

    def greet(step, carry):
        other, where = partner(step)

        @pl.when(i_work | works(other))
        def _():
            pl.semaphore_signal(
                barrier, inc=1, device_id=where, device_id_type=pl.DeviceIdType.MESH
            )

        return carry

    each_partner(greet)

    for load in loads:
        load.start()

    loads[0].wait()
    loads[1].wait()

    sub = iota((slots, slots), 0)
    lane = iota((slots, slots), 1)
    w_row = weight_ref[...].astype(F32)
    w_col = jnp.sum(jnp.where(sub == lane, w_row, 0.0), axis=1, keepdims=True)
    ends = ends_ref[...].astype(F32)
    end_row = [ends[e:e + 1] for e in range(2)]
    end_col = [
        jnp.sum(jnp.where(sub == lane, row, 0.0), axis=1, keepdims=True) for row in end_row
    ]
    live_row = jnp.where(w_row > 0, 1.0, 0.0)
    live_col = jnp.where(w_col > 0, 1.0, 0.0)
    rank_row = jnp.sum(jnp.where(sub < lane, live_col, 0.0), axis=0, keepdims=True)
    rank_col = jnp.sum(jnp.where(lane < sub, live_row, 0.0), axis=1, keepdims=True)
    rank_row = jnp.where(w_row > 0, rank_row, -1.0)
    rank_col = jnp.where(w_col > 0, rank_col, -1.0)

    loads[2].wait()
    image_stack = jnp.concatenate(
        [img[:, c * LANES:(c + 1) * LANES] for c in range(col_blocks)], axis=0
    )
    per_tile = LANES // imgs

    def fill(ch):
        row = iota((block, 1), 0)
        place = (row // ROWS + ch * ROWS).astype(F32)
        kind = row % ROWS
        chosen = jnp.where(kind >= col_blocks, end_row[1], end_row[0])
        image = jnp.sum(jnp.where(rank_row == place, chosen, 0.0), axis=1, keepdims=True)
        column = jnp.where(kind >= col_blocks, kind - col_blocks, kind)
        column = jnp.where(kind >= 2 * col_blocks, -1, column)
        across = iota((1, LANES), 1)
        which = (across % imgs).astype(F32)
        parts = [
            onehot((image == which) & (column == m * per_tile + across // imgs))
            for m in range(col_blocks // per_tile)
        ]
        picked = dot(jnp.concatenate(parts, axis=1), image_stack)
        send[rows_at(ch * block, block), :] = picked.astype(BF16)

    each_chunk(chunks, fill)

    @pl.when(i_work)
    def _():
        pl.semaphore_wait(barrier, n - 1)

    @pl.when(jnp.logical_not(i_work))
    def _():
        pl.semaphore_wait(barrier, workers)

    def move(source, target, where, which):
        pltpu.make_async_remote_copy(
            src_ref=source,
            dst_ref=target,
            send_sem=send_sem.at[which],
            recv_sem=recv_sem.at[which],
            device_id=where,
            device_id_type=pl.DeviceIdType.MESH,
        ).start()

    def await_blocks(blocks, sem):
        whole = recv.at[pl.ds(0, blocks * ROWS)]
        pltpu.make_async_copy(whole, whole, sem).wait()

    def send_tokens(step, carry):
        other, where = partner(step)

        @pl.when(works(other))
        def _():
            for q in range(2):
                move(
                    send.at[rows_at((2 * (other - first) + q) * ROWS, ROWS)],
                    recv.at[rows_at(q * n * ROWS + me * ROWS, ROWS)], where, 0,
                )

        return carry

    def send_messages(step, carry):
        other, where = partner(step)
        for q in range(2):
            move(
                send2.at[rows_at(q * n * ROWS + other * ROWS, ROWS)],
                recv2.at[rows_at((2 * (me - first) + q) * ROWS, ROWS)], where, 1,
            )
        return carry

    each_partner(send_tokens)

    def fill_combine(ch):
        across = iota((1, block), 1)
        place = (across // ROWS + ch * ROWS).astype(F32)
        kind = across % ROWS
        chosen = jnp.where(kind >= col_blocks, end_col[1], end_col[0])
        image = jnp.sum(jnp.where(rank_col == place, chosen, 0.0), axis=0, keepdims=True)
        column = jnp.where(kind >= col_blocks, kind - col_blocks, kind)
        column = jnp.where(kind >= 2 * col_blocks, -1, column)
        same = image == iota((imgs, 1), 0).astype(F32)
        for c in range(col_blocks):
            combine[ch, c * imgs:(c + 1) * imgs, :] = onehot(same & (column == c))

    each_chunk(chunks, fill_combine)
    number = iota((imgs, 1), 0).astype(F32)
    totals = 1.0 + jnp.sum(
        jnp.where(end_row[0] == number, w_row, 0.0) + jnp.where(end_row[1] == number, w_row, 0.0),
        axis=1, keepdims=True,
    )
    my_weight = [
        jnp.sum(
            jnp.where(rank_row == (2 * (me - first) + q).astype(F32), w_row, 0.0),
            axis=1, keepdims=True,
        )
        for q in range(2)
    ]
    height = 2 * ROWS * col_blocks

    def spot(row):
        return (row % ROWS) * ROWS + (row // ROWS % 2) * col_blocks + row // (2 * ROWS)

    unpack = onehot(spot(iota((height, 1), 0)) == iota((1, block), 1))
    pack = onehot(spot(iota((1, height), 1)) == iota((block, 1), 0))
    head_of = iota((1, 4 * HDIM), 1) // HDIM
    heads = [onehot(head_of == h) for h in range(4)]
    heads32 = [jnp.where(head_of == h, 1.0, 0.0) for h in range(4)]

    loads[3].wait()

    @pl.when(i_work)
    def _():
        for q in range(2):
            recv[rows_at(q * n * ROWS + me * ROWS, ROWS), :] = (
                send[rows_at((2 * (me - first) + q) * ROWS, ROWS), :]
            )
        await_blocks(2 * (n - 1), recv_sem.at[0])

        def project(ch):
            both = []
            for q in range(2):
                tokens = dot(unpack, recv[rows_at(q * n * ROWS + ch * block, block), :]).astype(BF16)
                both.append(jnp.concatenate(
                    [tokens[c * 2 * ROWS:(c + 1) * 2 * ROWS] for c in range(col_blocks)], axis=1
                ))
            tokens = jnp.concatenate(both, axis=0)
            for part in range(3):
                result = dot(tokens, wq[:, part * d:(part + 1) * d]).astype(BF16)
                for e in range(4):
                    proj[rows_at(e * n + ch * ROWS, ROWS), part * d:(part + 1) * d] = (
                        result[e * ROWS:(e + 1) * ROWS]
                    )

        each_chunk(chunks, project)

        group = iota((16 * ROWS, 1), 0) // ROWS % 4
        allowed = group + 1 - 2 * (group % 2) == iota((1, 4 * n), 1) // n

        def attend(ch):
            for b in range(d // (4 * HDIM)):
                lo = b * 4 * HDIM
                hi = lo + 4 * HDIM
                query = jnp.concatenate(
                    [proj[rows_at(own * n + ch * ROWS, ROWS), lo:hi] for own in range(4)], axis=0
                )
                split = jnp.concatenate([query * mask for mask in heads], axis=0)
                scores = lax.dot_general(
                    split, proj[:, d + lo:d + hi], (((1,), (1,)), ((), ())),
                    preferred_element_type=F32,
                ) * HDIM ** (-0.5)
                scores = jnp.where(allowed, scores, -jnp.inf)
                largest = jnp.max(scores, axis=1, keepdims=True)
                exponent = jnp.exp(scores - largest)
                total = jnp.sum(exponent, axis=1, keepdims=True)
                softmax = (exponent / total).astype(BF16)
                blended = dot(softmax, proj[:, 2 * d + lo:2 * d + hi])
                for own in range(4):
                    attended = sum(
                        blended[(4 * h + own) * ROWS:(4 * h + own + 1) * ROWS] * heads32[h]
                        for h in range(4)
                    )
                    message = (attended * my_weight[own // 2]).astype(BF16)
                    for half in range(2):
                        row = (own // 2) * height + ((2 * b + half) * 2 + own % 2) * ROWS
                        stack[row:row + ROWS, :] = message[:, half * LANES:(half + 1) * LANES]
            for q in range(2):
                send2[rows_at(q * n * ROWS + ch * block, block), :] = dot(
                    pack, stack[q * height:(q + 1) * height]
                ).astype(BF16)

        each_chunk(chunks, attend)
        each_partner(send_messages)
        for q in range(2):
            recv2[rows_at((2 * (me - first) + q) * ROWS, ROWS), :] = (
                send2[rows_at(q * n * ROWS + me * ROWS, ROWS), :]
            )
        await_blocks(2 * (workers - 1), send_sem.at[0])
        await_blocks(2 * (workers - 1), recv_sem.at[1])

    @pl.when(jnp.logical_not(i_work))
    def _():
        await_blocks(2 * workers, send_sem.at[0])
        await_blocks(2 * workers, recv_sem.at[1])

    def add_up(ch):
        return dot(combine[ch], recv2[rows_at(ch * block, block), :])

    if chunks == 1:
        summed = add_up(0)
    else:
        summed = lax.fori_loop(
            1, chunks, lambda ch, total: total + add_up(ch), add_up(0)
        )
    average = jnp.concatenate(
        [(summed[c * imgs:(c + 1) * imgs] / totals).astype(BF16) for c in range(col_blocks)],
        axis=1,
    )
    out_ref[...] = average

    @pl.when(i_work)
    def _():
        await_blocks(2 * (n - 1), send_sem.at[1])


def local(images, w_qkv, w_out, pair_list, pair_weight):
    row_devices = lax.axis_size("rows")
    n = lax.axis_size("pairs") * row_devices
    imgs, local_tokens, d = images.shape
    assert local_tokens == 1 and n % ROWS == 0
    slots = pair_list.shape[0]
    any_space = pl.BlockSpec(memory_space=pl.ANY)
    vmem = pl.BlockSpec(memory_space=pltpu.VMEM)
    col_blocks = d // LANES
    buffer = pltpu.VMEM((n * ROWS, LANES), BF16)
    twice = pltpu.VMEM((2 * n * ROWS, LANES), BF16)
    flat = images.reshape(imgs, d)
    result = pl.pallas_call(
        functools.partial(kernel, n, row_devices),
        out_shape=pltpu.VMEM((imgs, d), BF16),
        in_specs=[any_space] * 4,
        out_specs=vmem,
        scratch_shapes=[
            pltpu.VMEM((2, slots), jnp.int32),
            pltpu.VMEM((1, slots), jnp.int32),
            pltpu.VMEM((imgs, d), BF16),
            pltpu.VMEM(w_qkv.shape, BF16),
            buffer, twice, twice, buffer,
            pltpu.VMEM((4 * n, 3 * d), BF16),
            pltpu.VMEM((4 * ROWS * col_blocks, LANES), BF16),
            pltpu.VMEM((n // ROWS, imgs * col_blocks, ROWS * ROWS), BF16),
            pltpu.SemaphoreType.DMA((4,)),
            pltpu.SemaphoreType.DMA((2,)),
            pltpu.SemaphoreType.DMA((2,)),
        ],
        compiler_params=pltpu.CompilerParams(
            collective_id=0, has_side_effects=True, vmem_limit_bytes=56 * 1024 * 1024
        ),
    )(flat, w_qkv, pair_list.T, pair_weight.reshape(1, slots))
    update = jnp.dot(result, w_out, preferred_element_type=F32)
    return (flat.astype(F32) + update).astype(BF16).reshape(images.shape)


def solution(mesh):
    in_specs = (P("groups", ("pairs", "rows"), None), P(), P(), P("groups", None), P("groups"))
    out_specs = P("groups", ("pairs", "rows"), None)
    return jax.shard_map(local, mesh=mesh, in_specs=in_specs, out_specs=out_specs, check_vma=False)
```

```python
import functools

import jax
import jax.numpy as jnp
from jax import lax
from jax.experimental import pallas as pl
from jax.experimental.pallas import tpu as pltpu
from jax.sharding import PartitionSpec as P

HDIM = 64
LANES = 128
ROWS = 16
F32 = jnp.float32
BF16 = jnp.bfloat16


def iota(shape, axis):
    return lax.broadcasted_iota(jnp.int32, shape, axis)


def onehot(mask):
    return jnp.where(mask, 1.0, 0.0).astype(BF16)


def dot(a, b):
    return jnp.dot(a, b, preferred_element_type=F32)


def each_chunk(count, body):
    if count == 1:
        body(0)
    else:
        lax.fori_loop(0, count, lambda i, c: (body(i), c)[1], 0)


def rows_at(start, size):
    if isinstance(start, int):
        return pl.ds(start, size)
    return pl.ds(pl.multiple_of(start, ROWS), size)


def kernel(
    n, row_devices, img_hbm, wq_hbm, ends_hbm, weight_hbm, out_ref,
    ends_ref, weight_ref, img, wq, send, recv, send2, recv2, proj, stack, combine,
    load_sem, send_sem, recv_sem,
):
    imgs, d = img.shape
    slots = ends_ref.shape[1]
    col_blocks = d // LANES
    chunks = n // ROWS
    block = ROWS * ROWS
    pairs_pos = lax.axis_index("pairs")
    rows_pos = lax.axis_index("rows")
    me = pairs_pos * row_devices + rows_pos

    pairs_of_refs = [
        (ends_hbm, ends_ref), (weight_hbm, weight_ref), (img_hbm, img), (wq_hbm, wq)
    ]
    loads = [
        pltpu.make_async_copy(src, dst, load_sem.at[i])
        for i, (src, dst) in enumerate(pairs_of_refs)
    ]

    def partner(step):
        other = me
        bit = 1
        while bit < n:
            other = other + (step // bit % 2) * (1 - 2 * (me // bit % 2)) * bit
            bit *= 2
        return other, {"pairs": other // row_devices, "rows": lax.rem(other, row_devices)}

    def each_partner(body):
        if chunks == 1:
            for step in range(n - 1, 0, -1):
                body(step, 0)
        else:
            lax.fori_loop(1, n, lambda i, c: body(n - i, c), 0)

    barrier = pltpu.get_barrier_semaphore()

    workers = n // 2
    first = n // 4

    def works(device):
        return (device >= first) & (device < first + workers)

    i_work = works(me)

    def greet(step, carry):
        other, where = partner(step)

        @pl.when(i_work | works(other))
        def _():
            pl.semaphore_signal(
                barrier, inc=1, device_id=where, device_id_type=pl.DeviceIdType.MESH
            )

        return carry

    each_partner(greet)

    for load in loads[:3]:
        load.start()

    @pl.when(i_work)
    def _():
        loads[3].start()

    loads[0].wait()
    loads[1].wait()

    sub = iota((slots, slots), 0)
    lane = iota((slots, slots), 1)
    w_row = weight_ref[...].astype(F32)
    w_col = jnp.sum(jnp.where(sub == lane, w_row, 0.0), axis=1, keepdims=True)
    ends = ends_ref[...].astype(F32)
    end_row = [ends[e:e + 1] for e in range(2)]
    end_col = [
        jnp.sum(jnp.where(sub == lane, row, 0.0), axis=1, keepdims=True) for row in end_row
    ]
    live_row = jnp.where(w_row > 0, 1.0, 0.0)
    live_col = jnp.where(w_col > 0, 1.0, 0.0)
    rank_row = jnp.sum(jnp.where(sub < lane, live_col, 0.0), axis=0, keepdims=True)
    rank_col = jnp.sum(jnp.where(lane < sub, live_row, 0.0), axis=1, keepdims=True)
    rank_row = jnp.where(w_row > 0, rank_row, -1.0)
    rank_col = jnp.where(w_col > 0, rank_col, -1.0)

    loads[2].wait()
    image_stack = jnp.concatenate(
        [img[:, c * LANES:(c + 1) * LANES] for c in range(col_blocks)], axis=0
    )
    per_tile = LANES // imgs

    def fill(ch):
        row = iota((block, 1), 0)
        place = (row // ROWS + ch * ROWS).astype(F32)
        kind = row % ROWS
        chosen = jnp.where(kind >= col_blocks, end_row[1], end_row[0])
        image = jnp.sum(jnp.where(rank_row == place, chosen, 0.0), axis=1, keepdims=True)
        column = jnp.where(kind >= col_blocks, kind - col_blocks, kind)
        column = jnp.where(kind >= 2 * col_blocks, -1, column)
        across = iota((1, LANES), 1)
        which = (across % imgs).astype(F32)
        parts = [
            onehot((image == which) & (column == m * per_tile + across // imgs))
            for m in range(col_blocks // per_tile)
        ]
        picked = dot(jnp.concatenate(parts, axis=1), image_stack)
        send[rows_at(ch * block, block), :] = picked.astype(BF16)

    each_chunk(chunks, fill)

    @pl.when(i_work)
    def _():
        pl.semaphore_wait(barrier, n - 1)

    @pl.when(jnp.logical_not(i_work))
    def _():
        pl.semaphore_wait(barrier, workers)

    def move(source, target, where, which):
        pltpu.make_async_remote_copy(
            src_ref=source,
            dst_ref=target,
            send_sem=send_sem.at[which],
            recv_sem=recv_sem.at[which],
            device_id=where,
            device_id_type=pl.DeviceIdType.MESH,
        ).start()

    def await_blocks(blocks, sem):
        whole = recv.at[pl.ds(0, blocks * ROWS)]
        pltpu.make_async_copy(whole, whole, sem).wait()

    def send_tokens(step, carry):
        other, where = partner(step)

        @pl.when(works(other))
        def _():
            for q in range(2):
                move(
                    send.at[rows_at((2 * (other - first) + q) * ROWS, ROWS)],
                    recv.at[rows_at(q * n * ROWS + me * ROWS, ROWS)], where, 0,
                )

        return carry

    def send_messages(step, carry):
        other, where = partner(step)
        for q in range(2):
            move(
                send2.at[rows_at(q * n * ROWS + other * ROWS, ROWS)],
                recv2.at[rows_at((2 * (me - first) + q) * ROWS, ROWS)], where, 1,
            )
        return carry

    each_partner(send_tokens)

    def fill_combine(ch):
        across = iota((1, block), 1)
        place = (across // ROWS + ch * ROWS).astype(F32)
        kind = across % ROWS
        chosen = jnp.where(kind >= col_blocks, end_col[1], end_col[0])
        image = jnp.sum(jnp.where(rank_col == place, chosen, 0.0), axis=0, keepdims=True)
        column = jnp.where(kind >= col_blocks, kind - col_blocks, kind)
        column = jnp.where(kind >= 2 * col_blocks, -1, column)
        same = image == iota((imgs, 1), 0).astype(F32)
        for c in range(col_blocks):
            combine[ch, c * imgs:(c + 1) * imgs, :] = onehot(same & (column == c))

    each_chunk(chunks, fill_combine)
    number = iota((imgs, 1), 0).astype(F32)
    totals = 1.0 + jnp.sum(
        jnp.where(end_row[0] == number, w_row, 0.0) + jnp.where(end_row[1] == number, w_row, 0.0),
        axis=1, keepdims=True,
    )
    my_weight = [
        jnp.sum(
            jnp.where(rank_row == (2 * (me - first) + q).astype(F32), w_row, 0.0),
            axis=1, keepdims=True,
        )
        for q in range(2)
    ]
    height = 2 * ROWS * col_blocks

    def spot(row):
        return (row % ROWS) * ROWS + (row // ROWS % 2) * col_blocks + row // (2 * ROWS)

    unpack = onehot(spot(iota((height, 1), 0)) == iota((1, block), 1))
    pack = onehot(spot(iota((1, height), 1)) == iota((block, 1), 0))
    head_of = iota((1, 4 * HDIM), 1) // HDIM
    heads = [onehot(head_of == h) for h in range(4)]
    heads32 = [jnp.where(head_of == h, 1.0, 0.0) for h in range(4)]

    @pl.when(i_work)
    def _():
        loads[3].wait()
        for q in range(2):
            recv[rows_at(q * n * ROWS + me * ROWS, ROWS), :] = (
                send[rows_at((2 * (me - first) + q) * ROWS, ROWS), :]
            )
        await_blocks(2 * (n - 1), recv_sem.at[0])

        def project(ch):
            both = []
            for q in range(2):
                tokens = dot(unpack, recv[rows_at(q * n * ROWS + ch * block, block), :]).astype(BF16)
                both.append(jnp.concatenate(
                    [tokens[c * 2 * ROWS:(c + 1) * 2 * ROWS] for c in range(col_blocks)], axis=1
                ))
            tokens = jnp.concatenate(both, axis=0)
            for part in range(3):
                result = dot(tokens, wq[:, part * d:(part + 1) * d]).astype(BF16)
                for e in range(4):
                    proj[rows_at(e * n + ch * ROWS, ROWS), part * d:(part + 1) * d] = (
                        result[e * ROWS:(e + 1) * ROWS]
                    )

        each_chunk(chunks, project)

        group = iota((16 * ROWS, 1), 0) // ROWS % 4
        allowed = group + 1 - 2 * (group % 2) == iota((1, 4 * n), 1) // n

        def attend(ch):
            for b in range(d // (4 * HDIM)):
                lo = b * 4 * HDIM
                hi = lo + 4 * HDIM
                query = jnp.concatenate(
                    [proj[rows_at(own * n + ch * ROWS, ROWS), lo:hi] for own in range(4)], axis=0
                )
                split = jnp.concatenate([query * mask for mask in heads], axis=0)
                scores = lax.dot_general(
                    split, proj[:, d + lo:d + hi], (((1,), (1,)), ((), ())),
                    preferred_element_type=F32,
                ) * HDIM ** (-0.5)
                scores = jnp.where(allowed, scores, -jnp.inf)
                largest = jnp.max(scores, axis=1, keepdims=True)
                exponent = jnp.exp(scores - largest)
                total = jnp.sum(exponent, axis=1, keepdims=True)
                softmax = (exponent / total).astype(BF16)
                blended = dot(softmax, proj[:, 2 * d + lo:2 * d + hi])
                for own in range(4):
                    attended = sum(
                        blended[(4 * h + own) * ROWS:(4 * h + own + 1) * ROWS] * heads32[h]
                        for h in range(4)
                    )
                    message = (attended * my_weight[own // 2]).astype(BF16)
                    for half in range(2):
                        row = (own // 2) * height + ((2 * b + half) * 2 + own % 2) * ROWS
                        stack[row:row + ROWS, :] = message[:, half * LANES:(half + 1) * LANES]
            for q in range(2):
                send2[rows_at(q * n * ROWS + ch * block, block), :] = dot(
                    pack, stack[q * height:(q + 1) * height]
                ).astype(BF16)

        each_chunk(chunks, attend)
        each_partner(send_messages)
        for q in range(2):
            recv2[rows_at((2 * (me - first) + q) * ROWS, ROWS), :] = (
                send2[rows_at(q * n * ROWS + me * ROWS, ROWS), :]
            )
        await_blocks(2 * (workers - 1), send_sem.at[0])
        await_blocks(2 * (workers - 1), recv_sem.at[1])

    @pl.when(jnp.logical_not(i_work))
    def _():
        await_blocks(2 * workers, send_sem.at[0])
        await_blocks(2 * workers, recv_sem.at[1])

    def add_up(ch):
        return dot(combine[ch], recv2[rows_at(ch * block, block), :])

    if chunks == 1:
        summed = add_up(0)
    else:
        summed = lax.fori_loop(
            1, chunks, lambda ch, total: total + add_up(ch), add_up(0)
        )
    average = jnp.concatenate(
        [(summed[c * imgs:(c + 1) * imgs] / totals).astype(BF16) for c in range(col_blocks)],
        axis=1,
    )
    out_ref[...] = average

    @pl.when(i_work)
    def _():
        await_blocks(2 * (n - 1), send_sem.at[1])


def local(images, w_qkv, w_out, pair_list, pair_weight):
    row_devices = lax.axis_size("rows")
    n = lax.axis_size("pairs") * row_devices
    imgs, local_tokens, d = images.shape
    assert local_tokens == 1 and n % ROWS == 0
    slots = pair_list.shape[0]
    any_space = pl.BlockSpec(memory_space=pl.ANY)
    vmem = pl.BlockSpec(memory_space=pltpu.VMEM)
    col_blocks = d // LANES
    buffer = pltpu.VMEM((n * ROWS, LANES), BF16)
    twice = pltpu.VMEM((2 * n * ROWS, LANES), BF16)
    flat = images.reshape(imgs, d)
    result = pl.pallas_call(
        functools.partial(kernel, n, row_devices),
        out_shape=pltpu.VMEM((imgs, d), BF16),
        in_specs=[any_space] * 4,
        out_specs=vmem,
        scratch_shapes=[
            pltpu.VMEM((2, slots), jnp.int32),
            pltpu.VMEM((1, slots), jnp.int32),
            pltpu.VMEM((imgs, d), BF16),
            pltpu.VMEM(w_qkv.shape, BF16),
            buffer, twice, twice, buffer,
            pltpu.VMEM((4 * n, 3 * d), BF16),
            pltpu.VMEM((4 * ROWS * col_blocks, LANES), BF16),
            pltpu.VMEM((n // ROWS, imgs * col_blocks, ROWS * ROWS), BF16),
            pltpu.SemaphoreType.DMA((4,)),
            pltpu.SemaphoreType.DMA((2,)),
            pltpu.SemaphoreType.DMA((2,)),
        ],
        compiler_params=pltpu.CompilerParams(
            collective_id=0, has_side_effects=True, vmem_limit_bytes=56 * 1024 * 1024
        ),
    )(flat, w_qkv, pair_list.T, pair_weight.reshape(1, slots))
    update = jnp.dot(result, w_out, preferred_element_type=F32)
    return (flat.astype(F32) + update).astype(BF16).reshape(images.shape)


def solution(mesh):
    in_specs = (P("groups", ("pairs", "rows"), None), P(), P(), P("groups", None), P("groups"))
    out_specs = P("groups", ("pairs", "rows"), None)
    return jax.shard_map(local, mesh=mesh, in_specs=in_specs, out_specs=out_specs, check_vma=False)
```
